128 devices in a mesh: dp: 16 (over x_hi, y, core), tensor: 8 (over x_lo, z).
Axes of the slice: x: 4 (x_hi: 2, x_lo: 2; x = x_hi * 2 + x_lo), y: 4, z: 4, core: 2. Of those that a mesh axis runs over, the one named last changes fastest.
Arguments:
- activations: bfloat16 [4096, 6144], P('dp'), may hold values from -22 to 22
- out_grads: bfloat16 [4096, 24576], P('dp', 'tensor'), may hold values from -22 to 22
- weight_grad: bfloat16 [6144, 24576], P('dp', 'tensor'), may hold values from -6 to 6
Outputs:
- preconditioned: bfloat16 [6144, 24576], P('dp', 'tensor')
The draws below stay inside these ranges and needn't reach their ends.
All inputs are finite; a program needn't handle non-finite values.
Results may differ from the reference program's by a relative error of at most 0.035.
Values may be sent and summed in bfloat16 or wider, within the bound.
No kernel may reach another device: no remote copies, remote signals or barrier semaphores. Data moves between devices by JAX's collectives and lax.ppermute only.
A program may use at most 192 MiB of HBM per device.

```python
import jax
import jax.numpy as jnp
from jax import lax

D = 6144
FF = 24576
BLK = 1536
TOK_DEV = 256
TOKENS = 4096
N_DP = 16


def scaled_table(key, rows, cols):
    key_base, key_cols = jax.random.split(key, 2)
    col_scale = jnp.exp(jax.random.uniform(key_cols, (1, cols), minval=0.0, maxval=1.15))
    base = jnp.clip(jax.random.normal(key_base, (rows, cols)), -5.0, 5.0)
    return (base * col_scale).astype(jnp.bfloat16)


def draw_activations(key, part):
    key = jax.random.fold_in(key, 11)
    return scaled_table(key, TOKENS, D)


def draw_out_grads(key, part):
    key = jax.random.fold_in(key, 23)
    return scaled_table(key, TOKENS, FF)


def levels(stream_key, extent, shards, smallest, top_value):
    def one(axis_at, blocks):
        heights = jax.random.uniform(jax.random.fold_in(jax.random.fold_in(stream_key, 6), axis_at), (blocks,), jnp.float32, smallest / len(shards), top_value / len(shards))
        return jnp.repeat(jnp.exp(heights), extent[axis_at] // blocks).reshape((-1,) + (1,) * (len(extent) - axis_at - 1))

    loudness = one(*shards[0])
    for cut in shards[1:]:
        loudness = loudness * one(*cut)
    return loudness


def centred(rng, shape, scale, reach, cuts=(), kind=jnp.bfloat16):
    factor_of = levels(rng, shape, cuts, -0.22, 0.18) if cuts else 1.0
    entries = jax.random.normal(rng, shape, jnp.float32) * scale * factor_of
    return jnp.minimum(jnp.maximum(entries, -reach), reach).astype(kind)


def setup_inputs(seed: int = 0) -> dict:
    splits = jax.random.split(jax.random.key(seed), 4)
    return {
        "activations": draw_activations(jax.random.fold_in(splits[3], 71), 0),
        "out_grads": draw_out_grads(jax.random.fold_in(splits[3], 71), 0),
        "weight_grad": centred(splits[2], (D, FF), 1.0, 6.0, ((0, 16), (1, 8))),
    }


def damped_pair(covar):
    identity = jnp.eye(BLK, dtype=jnp.float32)
    mean_diag = jnp.trace(covar) / BLK + 1e-6
    damped = (covar + mean_diag * identity).astype(jnp.bfloat16)
    scale = 1.0 / (2.0 * mean_diag)
    first = (2.0 * scale * identity - scale * scale * damped.astype(jnp.float32)).astype(jnp.bfloat16)
    return damped, first


def newton_full(covar):
    damped, first = damped_pair(covar)
    product = jnp.dot(first.astype(jnp.float32), damped.astype(jnp.float32), precision=lax.Precision.HIGHEST).astype(jnp.bfloat16)
    second = jnp.dot(product.astype(jnp.float32), first.astype(jnp.float32), precision=lax.Precision.HIGHEST)
    return (2.0 * first.astype(jnp.float32) - second).astype(jnp.bfloat16)


def block_covariances(data):
    blocks = data.shape[1] // BLK
    total = jnp.zeros((blocks, BLK, BLK), jnp.float32)
    for shard in range(N_DP):
        rows = data[shard * TOK_DEV:(shard + 1) * TOK_DEV].astype(jnp.float32).reshape(TOK_DEV, blocks, BLK)
        partial_cov = jnp.einsum("tkb,tkc->kbc", rows, rows, precision=lax.Precision.HIGHEST)
        rounded = lax.optimization_barrier(partial_cov.astype(jnp.bfloat16))
        total = total + rounded.astype(jnp.float32)
    return total / TOKENS


def reference(activations, out_grads, weight_grad):
    g_cov = block_covariances(out_grads)
    a_cov = block_covariances(activations)
    right_parts = []
    for block in range(FF // BLK):
        g_inverse = newton_full(g_cov[block])
        piece = weight_grad[:, block * BLK:(block + 1) * BLK].astype(jnp.float32)
        right_parts.append(jnp.dot(piece, g_inverse.astype(jnp.float32), precision=lax.Precision.HIGHEST).astype(jnp.bfloat16))
    right = jnp.concatenate(right_parts, axis=1)
    left_parts = []
    for block in range(D // BLK):
        a_inverse = newton_full(a_cov[block])
        piece = right[block * BLK:(block + 1) * BLK].astype(jnp.float32)
        left_parts.append(jnp.dot(a_inverse.astype(jnp.float32), piece, precision=lax.Precision.HIGHEST))
    return jnp.concatenate(left_parts, axis=0).astype(jnp.bfloat16)
```

```python
import jax
import jax.numpy as jnp
from jax import lax
from jax.experimental import pallas as pl
from jax.experimental.pallas import tpu as pltpu
from jax.sharding import PartitionSpec as P

BLK = 1536
TOKENS = 4096
TILE = 128
SIDE = BLK // TILE
UPPER = [(i, j) for i in range(SIDE) for j in range(i, SIDE)]
SLOTS = 80
PIECE = 5
AXES = ("dp", "tensor")
VMEM = 56 * 1024 * 1024


def moves(target):
    pairs = []
    for dp in range(16):
        for tp in range(8):
            x_hi, y, core = dp // 8, dp // 2 % 4, dp % 2
            x_lo, z = tp // 4, tp % 4
            x_hi, y, core, x_lo, z = target(x_hi, y, core, x_lo, z)
            there = (x_hi * 8 + y * 2 + core) * 8 + x_lo * 4 + z % 4
            pairs.append((dp * 8 + tp, there))
    return pairs


CORE = moves(lambda h, y, c, l, z: (h, y, c ^ 1, l, z))
Y_NEAR = moves(lambda h, y, c, l, z: (h, y ^ 1, c, l, z))
Y_NEAR_CORE = moves(lambda h, y, c, l, z: (h, y ^ 1, c ^ 1, l, z))
Y_FAR = moves(lambda h, y, c, l, z: (h, y ^ 3, c, l, z))
X_HALF = moves(lambda h, y, c, l, z: (h ^ 1, y, c, l, z))
X_NEAR = moves(lambda h, y, c, l, z: (h, y, c, l ^ 1, z))
Z_UP = moves(lambda h, y, c, l, z: (h, y, c, l, z + 1))
Z_DOWN = moves(lambda h, y, c, l, z: (h, y, c, l, z + 3))
Z_HALF = moves(lambda h, y, c, l, z: (h, y, c, l, z + 2))


def send(array, pairs):
    return lax.ppermute(array, AXES, pairs)


def add(first, second):
    return (first.astype(jnp.float32) + second.astype(jnp.float32)).astype(jnp.bfloat16)


def place():
    dp, tp = lax.axis_index("dp"), lax.axis_index("tensor")
    return dp // 8, dp // 2 % 4, dp % 2, tp // 4, tp % 4


def slot_first(piece, code):
    rel = piece ^ code
    return rel ^ (rel >> 1 & 1)


def slot_second(piece, code):
    rel = piece ^ code
    low, mid, high = rel & 1, rel >> 1 & 1, rel >> 2
    return mid << 2 | (low ^ mid) << 1 | high


def slot_of(tile, code):
    piece, at = tile // PIECE, tile % PIECE
    if piece < 8:
        return slot_first(piece, code) * PIECE + at
    return (slot_second(piece - 8, code) + 8) * PIECE + at


def cov_g(own, got, first_send, second_send, first_keep, second_keep, tokens, packed, sems):
    x_hi, y, core, _, _ = place()
    half = own.shape[0]
    loads = [
        pltpu.make_async_copy(
            own.at[:, pl.ds(pl.multiple_of(core * BLK, BLK), BLK)], tokens.at[pl.ds(0, half)], sems.at[0]
        ),
        pltpu.make_async_copy(got, tokens.at[pl.ds(half, half)], sems.at[1]),
    ]
    for load in loads:
        load.start()
    for load in loads:
        load.wait()
    code = x_hi * 4 + y
    for row in range(SIDE // 2):
        start = row * 2 * TILE
        product = lax.dot_general(
            tokens[:, start : start + 2 * TILE],
            tokens[:, start:],
            (((0,), (0,)), ((), ())),
            preferred_element_type=jnp.float32,
        ).astype(jnp.bfloat16)
        for tile, (i, j) in enumerate(UPPER):
            if i // 2 == row:
                top, left = (i - 2 * row) * TILE, (j - 2 * row) * TILE
                packed[slot_of(tile, code)] = product[top : top + TILE, left : left + TILE]
    for tile in range(len(UPPER), SLOTS):
        packed[slot_of(tile, code)] = jnp.zeros((TILE, TILE), jnp.bfloat16)
    count = 4 * PIECE
    stores = [
        pltpu.make_async_copy(packed.at[pl.ds(at * count, count)], out, sems.at[2 + at])
        for at, out in ((1, first_send), (3, second_send), (0, first_keep), (2, second_keep))
    ]
    for store in stores:
        store.start()
    for store in stores:
        store.wait()


def cov_a(rows, cols, tokens, sent, kept):
    x_hi, y, core, x_lo, z = place()
    tp = x_lo * 4 + z
    own = x_hi * 2 + y // 2
    for out, side in ((sent, 1 - core), (kept, core)):
        for at in range(PIECE):
            tile = (tp * 2 + side) * PIECE + at
            i, j = rows[tile], cols[tile]
            for rel in range(4):
                start = (own ^ rel) * SIDE
                lhs = tokens[:, pl.ds(pl.multiple_of((start + i) * TILE, TILE), TILE)]
                rhs = tokens[:, pl.ds(pl.multiple_of((start + j) * TILE, TILE), TILE)]
                out[rel * PIECE + at] = lax.dot_general(
                    lhs, rhs, (((0,), (0,)), ((), ())), preferred_element_type=jnp.float32
                ).astype(jnp.bfloat16)


def spread(packed, slots, full):
    row = lax.broadcasted_iota(jnp.int32, (TILE, TILE), 0)
    col = lax.broadcasted_iota(jnp.int32, (TILE, TILE), 1)
    diagonal = jnp.zeros((TILE, TILE), jnp.float32)
    for tile, (i, j) in enumerate(UPPER):
        value = packed[slots(tile)]
        full[i * TILE : (i + 1) * TILE, j * TILE : (j + 1) * TILE] = value
        if i == j:
            diagonal = diagonal + value.astype(jnp.float32)
        else:
            full[j * TILE : (j + 1) * TILE, i * TILE : (i + 1) * TILE] = value.T
    return jnp.sum(jnp.where(row == col, diagonal, 0.0))


def scales(trace):
    mean = trace / (TOKENS * BLK) + 1e-06
    return 1.0 / (TOKENS * mean), 1.0 / (2.0 * mean)


STEP = 256


def newton_chain(full, ratio, scale, start_of, second, third, finish):
    @pl.loop(0, BLK // STEP)
    def _(at):
        cols = pl.ds(pl.multiple_of(at * STEP, STEP), STEP)
        second[:, cols] = start_of(cols).astype(jnp.bfloat16)

    @pl.loop(0, BLK // STEP)
    def _(at):
        cols = pl.ds(pl.multiple_of(at * STEP, STEP), STEP)
        turned = jnp.dot(second[...], full[:, cols], preferred_element_type=jnp.float32)
        third[:, cols] = (second[:, cols].astype(jnp.float32) + ratio * turned).astype(jnp.bfloat16)

    @pl.loop(0, BLK // STEP)
    def _(at):
        cols = pl.ds(pl.multiple_of(at * STEP, STEP), STEP)
        turned = jnp.dot(third[...], full[:, cols], preferred_element_type=jnp.float32)
        value = 2.0 * second[:, cols].astype(jnp.float32) - 0.75 * third[:, cols].astype(jnp.float32)
        finish(cols, (scale * (value + 0.25 * ratio * turned)).astype(jnp.bfloat16))


def left_kernel(*refs):
    parts, (w_own, w_core, w_near, w_cross, out) = refs[:8], refs[8:13]
    packed, full, second, third, inverse, weights, sems = refs[13:]
    x_hi, y, core, x_lo, z = place()
    low = y % 2
    count = 2 * PIECE
    copies = [
        pltpu.make_async_copy(part, packed.at[pl.ds(at * count, count)], sems.at[at])
        for at, part in enumerate(parts)
    ]
    rows = w_core.shape[0]
    own = w_own.at[:, pl.ds(pl.multiple_of(core * BLK, BLK), BLK)]
    for at, (source, side, lane) in enumerate(
        ((own, low, core), (w_core, low, 1 - core), (w_near, 1 - low, core), (w_cross, 1 - low, 1 - core))
    ):
        there = pl.multiple_of((side * 2 + lane) * rows, rows)
        copies.append(pltpu.make_async_copy(source, weights.at[pl.ds(there, rows)], sems.at[8 + at]))
    for copy in copies:
        copy.start()
    for copy in copies[:8]:
        copy.wait()

    def slots(tile):
        piece, at = tile // PIECE, tile % PIECE
        side, z_at, x_at = piece % 2, piece // 2 % 4, piece // 8
        return (((side ^ core) * 4 + (z_at - z + 4) % 4) * 2 + (x_at ^ x_lo)) * PIECE + at

    ratio, scale = scales(spread(packed, slots, full))
    first_row = pl.multiple_of(low * 2 * rows, 2 * rows)
    mine = pl.ds(first_row, 2 * rows)

    def start_of(cols):
        row = lax.broadcasted_iota(jnp.int32, (2 * rows, STEP), 0) + first_row
        col = lax.broadcasted_iota(jnp.int32, (2 * rows, STEP), 1) + cols.start
        return jnp.where(row == col, 1.5, 0.0) - 0.5 * ratio * full[mine, cols].astype(jnp.float32)

    def finish(cols, value):
        inverse[:, cols] = value

    newton_chain(full, ratio, scale, start_of, second, third, finish)
    for copy in copies[8:]:
        copy.wait()

    @pl.loop(0, BLK // STEP)
    def _(at):
        cols = pl.ds(pl.multiple_of(at * STEP, STEP), STEP)
        out[:, cols] = jnp.dot(
            inverse[...], weights[:, cols], preferred_element_type=jnp.float32
        ).astype(jnp.bfloat16)


def right_kernel(first_own, first_got, second_own, second_got, left, out, packed, full, second, third, sems):
    x_hi, y, _, _, _ = place()
    code = x_hi * 4 + y
    count = 4 * PIECE
    copies = [
        pltpu.make_async_copy(part, packed.at[pl.ds(at * count, count)], sems.at[at])
        for at, part in enumerate((first_own, first_got, second_own, second_got))
    ]
    for copy in copies:
        copy.start()
    for copy in copies:
        copy.wait()
    ratio, scale = scales(spread(packed, lambda tile: slot_of(tile, code), full))

    def start_of(cols):
        turned = jnp.dot(left[...], full[:, cols], preferred_element_type=jnp.float32)
        return 1.5 * left[:, cols].astype(jnp.float32) - 0.5 * ratio * turned

    def finish(cols, value):
        out[:, cols] = value

    newton_chain(full, ratio, scale, start_of, second, third, finish)


def whole(memory):
    return pl.BlockSpec(memory_space=memory)


def tiles(count):
    return jax.ShapeDtypeStruct((count, TILE, TILE), jnp.bfloat16)


def matrix(rows, cols):
    return pltpu.VMEM((rows, cols), jnp.bfloat16)


def on_device(activations, out_grads, weight_grad):
    rows = weight_grad.shape[0]
    core = lax.axis_index("dp") % 2
    other = (1 - core) * BLK
    params = pltpu.CompilerParams(vmem_limit_bytes=VMEM)

    w_other = lax.dynamic_slice_in_dim(weight_grad, other, BLK, 1)
    w_mine = lax.dynamic_slice_in_dim(weight_grad, core * BLK, BLK, 1)
    g_other = lax.dynamic_slice_in_dim(out_grads, other, BLK, 1)
    g_got = send(g_other, CORE)
    w_near = send(w_mine, Y_NEAR)
    w_cross = send(w_other, Y_NEAR_CORE)
    w_core = send(w_other, CORE)

    pairs = UPPER + [(0, 0)] * (SLOTS - len(UPPER))
    a_sent, a_kept = pl.pallas_call(
        cov_a,
        out_shape=[tiles(4 * PIECE)] * 2,
        in_specs=[whole(pltpu.SMEM)] * 2 + [whole(pltpu.VMEM)],
        out_specs=[whole(pltpu.VMEM)] * 2,
        compiler_params=params,
        cost_estimate=pl.CostEstimate(flops=40 * 2 * 256 * TILE * TILE, bytes_accessed=5 << 20, transcendentals=0),
        name="cov_a",
    )(
        jnp.array([i for i, _ in pairs], jnp.int32),
        jnp.array([j for _, j in pairs], jnp.int32),
        activations,
    )
    first_send, second_send, first_keep, second_keep = pl.pallas_call(
        cov_g,
        out_shape=[tiles(4 * PIECE)] * 4,
        in_specs=[whole(pl.ANY)] * 2,
        out_specs=[whole(pl.ANY)] * 4,
        scratch_shapes=[
            matrix(2 * out_grads.shape[0], BLK),
            pltpu.VMEM((SLOTS, TILE, TILE), jnp.bfloat16),
            pltpu.SemaphoreType.DMA((6,)),
        ],
        compiler_params=params,
        cost_estimate=pl.CostEstimate(flops=21 * 2 * 512 * 256 * 256, bytes_accessed=4 << 20, transcendentals=0),
        name="cov_g",
    )(out_grads, g_got)

    n = PIECE
    first_got = send(first_send, X_HALF)
    second_got = send(second_send, Y_FAR)
    a_sum = add(a_kept, send(a_sent, CORE))
    a_x = send(a_sum[2 * n :], X_HALF)

    first_next = send(add(first_keep[2 * n :], first_got[2 * n :]), Y_FAR)
    second_next = send(add(second_keep[2 * n :], second_got[2 * n :]), Y_NEAR)
    first_sum = add(first_keep[: 2 * n], first_got[: 2 * n])
    second_sum = add(second_keep[: 2 * n], second_got[: 2 * n])
    a_half = add(a_sum[: 2 * n], a_x)
    a_y = send(a_half[n:], Y_FAR)

    first_last = send(add(first_sum[n:], first_next[n:]), Y_NEAR)
    second_last = send(add(second_sum[n:], second_next[n:]), X_HALF)
    first_own = add(add(first_sum[:n], first_next[:n]), first_last)
    second_own = add(add(second_sum[:n], second_next[:n]), second_last)
    a_quarter = add(a_half[:n], a_y)
    a_own = add(a_quarter, send(a_quarter, Y_NEAR))

    first_own = jnp.concatenate([first_own, send(first_own, Y_NEAR)])
    second_own = jnp.concatenate([second_own, send(second_own, X_HALF)])
    a_own = jnp.concatenate([a_own, send(a_own, X_NEAR)])
    first_own = jnp.concatenate([first_own, send(first_own, Y_FAR)])
    second_own = jnp.concatenate([second_own, send(second_own, Y_NEAR)])
    a_parts = [a_own, send(a_own, Z_DOWN), send(a_own, Z_HALF), send(a_own, Z_UP)]
    first_got = send(first_own, X_HALF)
    second_got = send(second_own, Y_FAR)
    a_parts = a_parts + [send(part, CORE) for part in a_parts]

    left = pl.pallas_call(
        left_kernel,
        out_shape=jax.ShapeDtypeStruct((2 * rows, BLK), jnp.bfloat16),
        in_specs=[whole(pl.ANY)] * 12,
        out_specs=whole(pltpu.VMEM),
        scratch_shapes=[
            pltpu.VMEM((SLOTS, TILE, TILE), jnp.bfloat16),
            matrix(BLK, BLK),
            matrix(2 * rows, BLK),
            matrix(2 * rows, BLK),
            matrix(2 * rows, BLK),
            matrix(BLK, BLK),
            pltpu.SemaphoreType.DMA((12,)),
        ],
        compiler_params=params,
        cost_estimate=pl.CostEstimate(flops=6 * 2 * rows * BLK * BLK, bytes_accessed=10 << 20, transcendentals=0),
        name="left",
    )(*a_parts, weight_grad, w_core, w_near, w_cross)
    block = pl.pallas_call(
        right_kernel,
        out_shape=jax.ShapeDtypeStruct((2 * rows, BLK), jnp.bfloat16),
        in_specs=[whole(pl.ANY)] * 4 + [whole(pltpu.VMEM)],
        out_specs=whole(pltpu.VMEM),
        scratch_shapes=[
            pltpu.VMEM((SLOTS, TILE, TILE), jnp.bfloat16),
            matrix(BLK, BLK),
            matrix(2 * rows, BLK),
            matrix(2 * rows, BLK),
            pltpu.SemaphoreType.DMA((4,)),
        ],
        compiler_params=params,
        cost_estimate=pl.CostEstimate(flops=6 * 2 * rows * BLK * BLK, bytes_accessed=8 << 20, transcendentals=0),
        name="right",
    )(first_own, first_got, second_own, second_got, left)
    mine = lax.dynamic_slice_in_dim(block, core * rows, rows, 0)
    theirs = send(lax.dynamic_slice_in_dim(block, (1 - core) * rows, rows, 0), CORE)
    return jnp.where(core == 0, jnp.concatenate([mine, theirs], 1), jnp.concatenate([theirs, mine], 1))


def solution(mesh):
    return jax.shard_map(
        on_device,
        mesh=mesh,
        in_specs=(P("dp", None), P("dp", "tensor"), P("dp", "tensor")),
        out_specs=P("dp", "tensor"),
        check_vma=False,
    )
```

```python
import jax
import jax.numpy as jnp
from jax import lax
from jax.experimental import pallas as pl
from jax.experimental.pallas import tpu as pltpu
from jax.sharding import PartitionSpec as P

BLK = 1536
TOKENS = 4096
TILE = 128
SIDE = BLK // TILE
UPPER = [(i, j) for i in range(SIDE) for j in range(i, SIDE)]
SLOTS = 80
PIECE = 10
WIDTH = 5
A_PIECE = 5
STEP = 256
CHUNKS = ((0, 0, 384), (1, 0, 64), (1, 64, 64), (1, 128, 256))
AXES = ("dp", "tensor")
MIB = 1024 * 1024


def moves(target):
    pairs = []
    for dp in range(16):
        for tp in range(8):
            x_hi, y, core = dp // 8, dp // 2 % 4, dp % 2
            x_lo, z = tp // 4, tp % 4
            x_hi, y, core, x_lo, z = target(x_hi, y, core, x_lo, z)
            there = (x_hi * 8 + y * 2 + core) * 8 + x_lo * 4 + z % 4
            pairs.append((dp * 8 + tp, there))
    return pairs


CORE = moves(lambda h, y, c, l, z: (h, y, c ^ 1, l, z))
Y_NEAR = moves(lambda h, y, c, l, z: (h, y ^ 1, c, l, z))
Y_NEAR_CORE = moves(lambda h, y, c, l, z: (h, y ^ 1, c ^ 1, l, z))
Y_FAR = moves(lambda h, y, c, l, z: (h, y ^ 3, c, l, z))
X_HALF = moves(lambda h, y, c, l, z: (h ^ 1, y, c, l, z))
X_Y_FAR = moves(lambda h, y, c, l, z: (h ^ 1, y ^ 3, c, l, z))
X_NEAR = moves(lambda h, y, c, l, z: (h, y, c, l ^ 1, z))
Z_UP = moves(lambda h, y, c, l, z: (h, y, c, l, z + 1))
Z_DOWN = moves(lambda h, y, c, l, z: (h, y, c, l, z + 3))
Z_HALF = moves(lambda h, y, c, l, z: (h, y, c, l, z + 2))


def send(array, pairs, name):
    with jax.named_scope(name):
        return lax.ppermute(array, AXES, pairs)


def together(*values):
    return lax.optimization_barrier(values)


def add(*terms):
    return sum(term.astype(jnp.float32) for term in terms).astype(jnp.bfloat16)


def swapped(array):
    half = array.shape[0] // 2
    return jnp.concatenate([array[half:], array[:half]])


def place():
    dp, tp = lax.axis_index("dp"), lax.axis_index("tensor")
    return dp // 8, dp // 2 % 4, dp % 2, tp // 4, tp % 4


def slot_first(piece, code):
    rel = piece ^ code
    return rel ^ (rel >> 1 & 1)


def slot_second(piece, code):
    rel = piece ^ code
    low, mid, high = rel & 1, rel >> 1 & 1, rel >> 2
    return mid << 2 | (low ^ mid) << 1 | high


def slot_of(tile, code, width):
    piece, at = tile // PIECE, tile % PIECE
    if at < width:
        return 0, slot_first(piece, code), at
    return 1, slot_second(piece, code), at - width


def cov_g(own, got, first_send, second_send, first_keep, second_keep, tokens):
    x_hi, y, core, _, _ = place()
    half = own.shape[0]
    tokens[:half] = own[:, pl.ds(pl.multiple_of(core * BLK, BLK), BLK)]
    tokens[half:] = got[...]
    code = x_hi * 4 + y
    sends, keeps = (first_send, second_send), (first_keep, second_keep)

    def store(tile, value):
        part, piece, at = slot_of(tile, code, WIDTH)
        count = (WIDTH, PIECE - WIDTH)[part]

        @pl.when(piece >= 4)
        def _():
            sends[part][(piece - 4) * count + at] = value

        @pl.when(piece < 4)
        def _():
            keeps[part][piece * count + at] = value

    for row in range(SIDE // 2):
        start = row * 2 * TILE
        product = lax.dot_general(
            tokens[:, start : start + 2 * TILE],
            tokens[:, start:],
            (((0,), (0,)), ((), ())),
            preferred_element_type=jnp.float32,
        ).astype(jnp.bfloat16)
        for tile, (i, j) in enumerate(UPPER):
            if i // 2 == row:
                top, left = (i - 2 * row) * TILE, (j - 2 * row) * TILE
                store(tile, product[top : top + TILE, left : left + TILE])
    for tile in range(len(UPPER), SLOTS):
        store(tile, jnp.zeros((TILE, TILE), jnp.bfloat16))


def corner(tile):
    starts = [i * SIDE - i * (i - 1) // 2 for i in range(SIDE)]
    i = sum((tile >= start).astype(jnp.int32) for start in starts[1:])
    return i, jnp.minimum(tile - (i * SIDE - i * (i - 1) // 2) + i, SIDE - 1)


def cov_a(whole_tokens, whole_weights, sent, kept, *refs):
    chunks, (tokens, sems) = refs[:-2], refs[-2:]
    x_hi, y, core, x_lo, z = place()
    tp = x_lo * 4 + z
    own = x_hi * 2 + y // 2
    loads = [
        pltpu.make_async_copy(
            whole_tokens.at[:, pl.ds(pl.multiple_of((own ^ rel) * BLK, BLK), BLK)], tokens.at[rel], sems.at[rel]
        )
        for rel in range(4)
    ]
    cuts = [
        pltpu.make_async_copy(
            whole_weights.at[pl.ds(start, count), pl.ds(pl.multiple_of((core ^ lane) * BLK, BLK), BLK)],
            chunk,
            sems.at[4 + at],
        )
        for at, ((lane, start, count), chunk) in enumerate(zip(CHUNKS[1:], chunks))
    ]
    for copy in loads + cuts:
        copy.start()
    for rel, load in enumerate(loads):
        load.wait()
        for out, side in ((sent, 1 - core), (kept, core)):
            for at in range(A_PIECE):
                i, j = corner((tp * 2 + side) * A_PIECE + at)
                left, right = (
                    tokens[rel, :, pl.ds(pl.multiple_of(place_of * TILE, TILE), TILE)] for place_of in (i, j)
                )
                out[rel * A_PIECE + at] = lax.dot_general(
                    left, right, (((0,), (0,)), ((), ())), preferred_element_type=jnp.float32
                ).astype(jnp.bfloat16)
    for copy in cuts:
        copy.wait()


def put(full, i, j, value):
    full[i * TILE : (i + 1) * TILE, j * TILE : (j + 1) * TILE] = value
    if i != j:
        full[j * TILE : (j + 1) * TILE, i * TILE : (i + 1) * TILE] = value.T


def diagonal_sum(full):
    row = lax.broadcasted_iota(jnp.int32, (TILE, TILE), 0)
    col = lax.broadcasted_iota(jnp.int32, (TILE, TILE), 1)
    total = jnp.zeros((TILE, TILE), jnp.float32)
    for at in range(0, BLK, TILE):
        total = total + full[at : at + TILE, at : at + TILE].astype(jnp.float32)
    return jnp.sum(jnp.where(row == col, total, 0.0))


def scales(trace):
    mean = trace / (TOKENS * BLK) + 1e-06
    return 1.0 / (TOKENS * mean), 1.0 / (2.0 * mean)


def steps():
    return [slice(at, at + STEP) for at in range(0, BLK, STEP)]


def dot(left, right):
    return jnp.dot(left, right, preferred_element_type=jnp.float32)


def newton_chain(full, ratio, scale, start_of, second, third, finish):
    for cols in steps():
        second[:, cols] = start_of(cols).astype(jnp.bfloat16)
    for cols in steps():
        turned = dot(second[...], full[:, cols])
        third[:, cols] = (second[:, cols].astype(jnp.float32) + ratio * turned).astype(jnp.bfloat16)
    for cols in steps():
        turned = dot(third[...], full[:, cols])
        value = 2.0 * second[:, cols].astype(jnp.float32) - 0.75 * third[:, cols].astype(jnp.float32)
        finish(cols, (scale * (value + 0.25 * ratio * turned)).astype(jnp.bfloat16))


def inverse_kernel(*refs):
    parts, out, packed, full, second, third = refs[:10], *refs[10:]
    _, y, core, x_lo, z = place()
    rows = out.shape[0]
    start = 0
    for part in parts:
        packed[start : start + part.shape[0]] = part[...]
        start += part.shape[0]
    for tile, (i, j) in enumerate(UPPER):
        piece, at = tile // A_PIECE, tile % A_PIECE
        side, z_at, x_at = piece % 2, piece // 2 % 4, piece // 8
        slot = (((side ^ core) * 4 + (z_at - z + 4) % 4) * 2 + (x_at ^ x_lo)) * A_PIECE + at
        put(full, i, j, packed[slot])
    ratio, scale = scales(diagonal_sum(full))
    first_row = pl.multiple_of(y % 2 * rows, rows)

    def start_of(cols):
        row = lax.broadcasted_iota(jnp.int32, (rows, STEP), 0) + first_row
        col = lax.broadcasted_iota(jnp.int32, (rows, STEP), 1) + cols.start
        return jnp.where(row == col, 1.5, 0.0) - 0.5 * ratio * full[pl.ds(first_row, rows), cols].astype(jnp.float32)

    def finish(cols, value):
        out[:, cols] = value

    newton_chain(full, ratio, scale, start_of, second, third, finish)


LATE = BLK // 4 - CHUNKS[-1][2]


def last_start(low, core):
    return pl.multiple_of(((1 - low) * 2 + 1 - core) * (BLK // 4), TILE)


def left_kernel(inverse, w_own, w_core, *refs):
    chunks, (out, weights) = refs[:-2], refs[-2:]
    _, y, core, _, _ = place()
    low = y % 2
    rows = w_core.shape[0]
    pieces = [(w_own.at[:, pl.ds(pl.multiple_of(core * BLK, BLK), BLK)], (low * 2 + core) * rows), (w_core, (low * 2 + 1 - core) * rows)]
    for chunk, (other, start, _) in zip(chunks, CHUNKS):
        lane = 1 - core if other else core
        pieces.append((chunk, ((1 - low) * 2 + lane) * rows + start))
    weights[pl.ds(last_start(low, core) + LATE, CHUNKS[-1][2])] = jnp.zeros((CHUNKS[-1][2], BLK), jnp.bfloat16)
    for piece, there in pieces:
        weights[pl.ds(pl.multiple_of(there, 64), piece.shape[0])] = piece[...]
    for cols in steps():
        out[:, cols] = dot(inverse[...], weights[:, cols])


def right_kernel(
    first_own, first_got, second_own, second_got, part_left, inverse, chunk, theirs, mine, full, left, second, third, late
):
    x_hi, y, core, _, _ = place()
    code = x_hi * 4 + y
    rows = mine.shape[0]
    owns, gots = (first_own, second_own), (first_got, second_got)
    for tile, (i, j) in enumerate(UPPER):
        part, piece, at = slot_of(tile, code, WIDTH)
        index = (piece & 3) * (WIDTH, PIECE - WIDTH)[part] + at
        put(full, i, j, jnp.where(piece >= 4, gots[part][index], owns[part][index]))
    ratio, scale = scales(diagonal_sum(full))

    late[:LATE] = jnp.zeros((LATE, BLK), jnp.bfloat16)
    late[LATE:] = chunk[...]
    last = pl.ds(last_start(y % 2, core), BLK // 4)
    for cols in steps():
        left[:, cols] = (part_left[:, cols] + dot(inverse[:, last], late[:, cols])).astype(jnp.bfloat16)

    def start_of(cols):
        turned = dot(left[...], full[:, cols])
        return 1.5 * left[:, cols].astype(jnp.float32) - 0.5 * ratio * turned

    def finish(cols, value):
        theirs[:, cols] = jnp.where(core == 0, value[rows:], value[:rows])
        mine[:, cols] = jnp.where(core == 0, value[:rows], value[rows:])

    newton_chain(full, ratio, scale, start_of, second, third, finish)


def whole(memory):
    return pl.BlockSpec(memory_space=memory)


def tiles(count):
    return jax.ShapeDtypeStruct((count, TILE, TILE), jnp.bfloat16)


def matrix(rows, cols):
    return pltpu.VMEM((rows, cols), jnp.bfloat16)


def shaped(rows, cols):
    return jax.ShapeDtypeStruct((rows, cols), jnp.bfloat16)


def kernel(body, name, operands, in_specs, out_shape, out_specs, scratch, flops, moved, vmem):
    return pl.pallas_call(
        body,
        out_shape=out_shape,
        in_specs=[whole(space) for space in in_specs],
        out_specs=jax.tree.map(whole, out_specs),
        scratch_shapes=scratch,
        compiler_params=pltpu.CompilerParams(vmem_limit_bytes=vmem * MIB),
        cost_estimate=pl.CostEstimate(flops=flops, bytes_accessed=moved, transcendentals=0),
        name=name,
    )(*operands)


def on_device(activations, out_grads, weight_grad):
    rows = weight_grad.shape[0]
    core = lax.axis_index("dp") % 2
    other = (1 - core) * BLK
    n, m, a = WIDTH, PIECE - WIDTH, A_PIECE

    g_other = lax.dynamic_slice_in_dim(out_grads, other, BLK, 1)
    w_0 = lax.dynamic_slice_in_dim(weight_grad, core * BLK, BLK, 1)
    g_other, w_0, activations = together(g_other, w_0, activations)
    g_got = send(g_other, CORE, "g_tokens")
    w_0 = send(w_0, Y_NEAR, "w_0")
    a_sent, a_kept, w_1, w_2, w_3 = kernel(
        cov_a,
        "cov_a",
        (activations, weight_grad),
        [pltpu.HBM, pltpu.HBM],
        [tiles(4 * a)] * 2 + [shaped(count, BLK) for _, _, count in CHUNKS[1:]],
        [pltpu.VMEM] * 2 + [pl.ANY] * (len(CHUNKS) - 1),
        [pltpu.VMEM((4, activations.shape[0], BLK), jnp.bfloat16), pltpu.SemaphoreType.DMA((3 + len(CHUNKS),))],
        40 * 2 * 256 * TILE * TILE,
        5 << 20,
        16,
    )
    a_swapped = send(a_sent, CORE, "a_core")

    a_swapped, g_got = together(a_swapped, g_got)
    a_sum = add(a_kept, a_swapped)
    a_parts = [a_sum[at * a : (at + 1) * a] for at in range(4)]
    a_both = send(a_parts[3], X_Y_FAR, "a_sum_both")
    a_x = send(a_parts[2], X_HALF, "a_sum_x")
    a_y = send(a_parts[1], Y_FAR, "a_sum_y")
    a_parts = [a_parts[0], a_y, a_x, a_both]
    first_send, second_send, first_keep, second_keep = kernel(
        cov_g,
        "cov_g",
        (out_grads, g_got),
        [pltpu.VMEM] * 2,
        [tiles(4 * n), tiles(4 * m), tiles(4 * n), tiles(4 * m)],
        [pltpu.VMEM] * 4,
        [matrix(2 * out_grads.shape[0], BLK)],
        21 * 2 * 512 * 256 * 256,
        4 << 20,
        16,
    )

    first_send, second_send, w_1, *a_parts = together(first_send, second_send, w_1, *a_parts)
    a_quarter = add(*a_parts)
    first_got = send(first_send, X_HALF, "sum_1_x")
    second_got = send(second_send, Y_FAR, "sum_1_y")
    a_near = send(a_quarter, Y_NEAR, "a_near")
    w_1 = send(w_1, Y_NEAR_CORE, "w_1")

    first_got, second_got, a_near, w_0, w_1 = together(first_got, second_got, a_near, w_0, w_1)
    first_next = send(add(first_keep[2 * n :], first_got[2 * n :]), Y_FAR, "sum_2_y")
    second_next = send(add(second_keep[2 * m :], second_got[2 * m :]), Y_NEAR, "sum_2_near")
    a_own = add(a_quarter, a_near)
    a_pair = send(a_own, X_NEAR, "a_pair")
    first_sum = add(first_keep[: 2 * n], first_got[: 2 * n])
    second_sum = add(second_keep[: 2 * m], second_got[: 2 * m])

    first_next, second_next, a_pair = together(first_next, second_next, a_pair)
    first_sum = add(first_sum, first_next)
    second_sum = add(second_sum, second_next)
    second_last = send(second_sum, X_HALF, "sum_3_x")
    first_last = send(first_sum, Y_NEAR, "sum_3_near")
    a_own = jnp.concatenate([a_own, a_pair])
    a_below, a_above = send(a_own, Z_UP, "a_up"), send(a_own, Z_DOWN, "a_down")

    first_last, second_last, w_2 = together(first_last, second_last, w_2)
    first_own = add(first_sum, swapped(first_last))
    second_own = add(second_sum, swapped(second_last))
    first_got = send(first_own, Y_FAR, "back_4_y")
    second_got = send(second_own, Y_NEAR, "back_4_near")
    a_far = [send(a_below[:a], Z_UP, "a_up_2"), send(a_above[a:], Z_DOWN, "a_down_2")]
    a_parts = (a_own, a_above, *a_far, a_below)
    a_swapped = [send(part, CORE, "a_core_back") for part in a_parts]
    w_core = send(lax.dynamic_slice_in_dim(weight_grad, other, BLK, 1), CORE, "w_core")
    w_2 = send(w_2, Y_NEAR_CORE, "w_2")

    first_got, second_got, w_core, w_2, w_3, a_own = together(first_got, second_got, w_core, w_2, w_3, a_own)
    first_own = jnp.concatenate([first_own, first_got])
    second_own = jnp.concatenate([second_own, second_got])
    first_got = send(first_own, X_HALF, "back_5_x")
    second_got = send(second_own, Y_FAR, "back_5_y")
    w_3 = send(w_3, Y_NEAR_CORE, "w_3")
    a_parts = (a_own, *a_parts[1:], *a_swapped)

    inverse = kernel(
        inverse_kernel,
        "inverse",
        a_parts,
        [pltpu.VMEM] * 10,
        shaped(2 * rows, BLK),
        pltpu.VMEM,
        [pltpu.VMEM((SLOTS, TILE, TILE), jnp.bfloat16), matrix(BLK, BLK), matrix(2 * rows, BLK), matrix(2 * rows, BLK)],
        4 * 2 * rows * BLK * BLK,
        5 << 20,
        24,
    )
    left = kernel(
        left_kernel,
        "left",
        (inverse, weight_grad, w_core, w_0, w_1, w_2),
        [pltpu.VMEM] * 6,
        jax.ShapeDtypeStruct((2 * rows, BLK), jnp.float32),
        pltpu.VMEM,
        [matrix(BLK, BLK)],
        2 * 2 * rows * BLK * BLK,
        9 << 20,
        20,
    )
    theirs, mine = kernel(
        right_kernel,
        "right",
        (first_own, first_got, second_own, second_got, left, inverse, w_3),
        [pltpu.VMEM] * 7,
        [shaped(rows, BLK)] * 2,
        [pltpu.VMEM] * 2,
        [matrix(BLK, BLK)] + [matrix(2 * rows, BLK)] * 3 + [matrix(rows, BLK)],
        6 * 2 * rows * BLK * BLK,
        8 << 20,
        24,
    )
    theirs = send(theirs, CORE, "out_core")
    return jnp.where(core == 0, jnp.concatenate([mine, theirs], 1), jnp.concatenate([theirs, mine], 1))


def solution(mesh):
    return jax.shard_map(
        on_device,
        mesh=mesh,
        in_specs=(P("dp", None), P("dp", "tensor"), P("dp", "tensor")),
        out_specs=P("dp", "tensor"),
        check_vma=False,
    )
```

```python
import jax
import jax.numpy as jnp
from jax import lax
from jax.experimental import pallas as pl
from jax.experimental.pallas import tpu as pltpu
from jax.sharding import PartitionSpec as P

BLK = 1536
TOKENS = 4096
TILE = 128
SIDE = BLK // TILE
UPPER = [(i, j) for i in range(SIDE) for j in range(i, SIDE)]
SLOTS = 80
PIECE = 10
WIDTH = 5
A_PIECE = 5
STEP = 256
CHUNKS = ((0, 0, 384), (1, 0, 64), (1, 64, 64), (1, 128, 256))
AXES = ("dp", "tensor")
MIB = 1024 * 1024


def moves(target):
    pairs = []
    for dp in range(16):
        for tp in range(8):
            x_hi, y, core = dp // 8, dp // 2 % 4, dp % 2
            x_lo, z = tp // 4, tp % 4
            x_hi, y, core, x_lo, z = target(x_hi, y, core, x_lo, z)
            there = (x_hi * 8 + y * 2 + core) * 8 + x_lo * 4 + z % 4
            pairs.append((dp * 8 + tp, there))
    return pairs


CORE = moves(lambda h, y, c, l, z: (h, y, c ^ 1, l, z))
Y_NEAR = moves(lambda h, y, c, l, z: (h, y ^ 1, c, l, z))
Y_NEAR_CORE = moves(lambda h, y, c, l, z: (h, y ^ 1, c ^ 1, l, z))
Y_FAR = moves(lambda h, y, c, l, z: (h, y ^ 3, c, l, z))
X_HALF = moves(lambda h, y, c, l, z: (h ^ 1, y, c, l, z))
X_Y_FAR = moves(lambda h, y, c, l, z: (h ^ 1, y ^ 3, c, l, z))
X_NEAR = moves(lambda h, y, c, l, z: (h, y, c, l ^ 1, z))
Z_UP = moves(lambda h, y, c, l, z: (h, y, c, l, z + 1))
Z_DOWN = moves(lambda h, y, c, l, z: (h, y, c, l, z + 3))
Z_HALF = moves(lambda h, y, c, l, z: (h, y, c, l, z + 2))


def send(array, pairs, name):
    with jax.named_scope(name):
        return lax.ppermute(array, AXES, pairs)


def together(*values):
    return lax.optimization_barrier(values)


def add(*terms):
    return sum(term.astype(jnp.float32) for term in terms).astype(jnp.bfloat16)


def swapped(array):
    half = array.shape[0] // 2
    return jnp.concatenate([array[half:], array[:half]])


def place():
    dp, tp = lax.axis_index("dp"), lax.axis_index("tensor")
    return dp // 8, dp // 2 % 4, dp % 2, tp // 4, tp % 4


def slot_first(piece, code):
    rel = piece ^ code
    return rel ^ (rel >> 1 & 1)


def slot_second(piece, code):
    rel = piece ^ code
    low, mid, high = rel & 1, rel >> 1 & 1, rel >> 2
    return mid << 2 | (low ^ mid) << 1 | high


def slot_of(tile, code, width):
    piece, at = tile // PIECE, tile % PIECE
    if at < width:
        return 0, slot_first(piece, code), at
    return 1, slot_second(piece, code), at - width


def cov_g(own, got, first_send, second_send, first_keep, second_keep, tokens):
    x_hi, y, core, _, _ = place()
    half = own.shape[0]
    tokens[:half] = own[:, pl.ds(pl.multiple_of(core * BLK, BLK), BLK)]
    tokens[half:] = got[...]
    code = x_hi * 4 + y
    sends, keeps = (first_send, second_send), (first_keep, second_keep)

    def store(tile, value):
        part, piece, at = slot_of(tile, code, WIDTH)
        count = (WIDTH, PIECE - WIDTH)[part]

        @pl.when(piece >= 4)
        def _():
            sends[part][(piece - 4) * count + at] = value

        @pl.when(piece < 4)
        def _():
            keeps[part][piece * count + at] = value

    for row in range(SIDE // 2):
        start = row * 2 * TILE
        product = lax.dot_general(
            tokens[:, start : start + 2 * TILE],
            tokens[:, start:],
            (((0,), (0,)), ((), ())),
            preferred_element_type=jnp.float32,
        ).astype(jnp.bfloat16)
        for tile, (i, j) in enumerate(UPPER):
            if i // 2 == row:
                top, left = (i - 2 * row) * TILE, (j - 2 * row) * TILE
                store(tile, product[top : top + TILE, left : left + TILE])
    for tile in range(len(UPPER), SLOTS):
        store(tile, jnp.zeros((TILE, TILE), jnp.bfloat16))


def corner(tile):
    starts = [i * SIDE - i * (i - 1) // 2 for i in range(SIDE)]
    i = sum((tile >= start).astype(jnp.int32) for start in starts[1:])
    return i, jnp.minimum(tile - (i * SIDE - i * (i - 1) // 2) + i, SIDE - 1)


def cov_a(whole_tokens, whole_weights, sent, kept, *refs):
    chunks, (tokens, sems) = refs[:-2], refs[-2:]
    x_hi, y, core, x_lo, z = place()
    tp = x_lo * 4 + z
    own = x_hi * 2 + y // 2
    loads = [
        pltpu.make_async_copy(
            whole_tokens.at[:, pl.ds(pl.multiple_of((own ^ rel) * BLK, BLK), BLK)], tokens.at[rel], sems.at[rel]
        )
        for rel in range(4)
    ]
    cuts = [
        pltpu.make_async_copy(
            whole_weights.at[pl.ds(start, count), pl.ds(pl.multiple_of((core ^ lane) * BLK, BLK), BLK)],
            chunk,
            sems.at[4 + at],
        )
        for at, ((lane, start, count), chunk) in enumerate(zip(CHUNKS[1:], chunks))
    ]
    for copy in loads + cuts:
        copy.start()
    for rel, load in enumerate(loads):
        load.wait()
        for out, side in ((sent, 1 - core), (kept, core)):
            for at in range(A_PIECE):
                i, j = corner((tp * 2 + side) * A_PIECE + at)
                left, right = (
                    tokens[rel, :, pl.ds(pl.multiple_of(place_of * TILE, TILE), TILE)] for place_of in (i, j)
                )
                out[rel * A_PIECE + at] = lax.dot_general(
                    left, right, (((0,), (0,)), ((), ())), preferred_element_type=jnp.float32
                ).astype(jnp.bfloat16)
    for copy in cuts:
        copy.wait()


def put(full, i, j, value):
    full[i * TILE : (i + 1) * TILE, j * TILE : (j + 1) * TILE] = value
    if i != j:
        full[j * TILE : (j + 1) * TILE, i * TILE : (i + 1) * TILE] = value.T


def diagonal_sum(full):
    row = lax.broadcasted_iota(jnp.int32, (TILE, TILE), 0)
    col = lax.broadcasted_iota(jnp.int32, (TILE, TILE), 1)
    total = jnp.zeros((TILE, TILE), jnp.float32)
    for at in range(0, BLK, TILE):
        total = total + full[at : at + TILE, at : at + TILE].astype(jnp.float32)
    return jnp.sum(jnp.where(row == col, total, 0.0))


def scales(trace):
    mean = trace / (TOKENS * BLK) + 1e-06
    return 1.0 / (TOKENS * mean), 1.0 / (2.0 * mean)


def steps():
    return [slice(at, at + STEP) for at in range(0, BLK, STEP)]


def dot(left, right):
    return jnp.dot(left, right, preferred_element_type=jnp.float32)


def newton_chain(full, ratio, scale, start_of, second, third, finish):
    for cols in steps():
        second[:, cols] = start_of(cols).astype(jnp.bfloat16)
    for cols in steps():
        turned = dot(second[...], full[:, cols])
        third[:, cols] = (second[:, cols].astype(jnp.float32) + ratio * turned).astype(jnp.bfloat16)
    for cols in steps():
        turned = dot(third[...], full[:, cols])
        value = 2.0 * second[:, cols].astype(jnp.float32) - 0.75 * third[:, cols].astype(jnp.float32)
        finish(cols, (scale * (value + 0.25 * ratio * turned)).astype(jnp.bfloat16))


def inverse_kernel(*refs):
    parts, out, packed, full, second, third = refs[:10], *refs[10:]
    _, y, core, x_lo, z = place()
    rows = out.shape[0]
    start = 0
    for part in parts:
        packed[start : start + part.shape[0]] = part[...]
        start += part.shape[0]
    for tile, (i, j) in enumerate(UPPER):
        piece, at = tile // A_PIECE, tile % A_PIECE
        side, z_at, x_at = piece % 2, piece // 2 % 4, piece // 8
        slot = (((side ^ core) * 4 + (z_at - z + 4) % 4) * 2 + (x_at ^ x_lo)) * A_PIECE + at
        put(full, i, j, packed[slot])
    ratio, scale = scales(diagonal_sum(full))
    first_row = pl.multiple_of(y % 2 * rows, rows)

    def start_of(cols):
        row = lax.broadcasted_iota(jnp.int32, (rows, STEP), 0) + first_row
        col = lax.broadcasted_iota(jnp.int32, (rows, STEP), 1) + cols.start
        return jnp.where(row == col, 1.5, 0.0) - 0.5 * ratio * full[pl.ds(first_row, rows), cols].astype(jnp.float32)

    def finish(cols, value):
        out[:, cols] = value

    newton_chain(full, ratio, scale, start_of, second, third, finish)


def last_start(low, core):
    return pl.multiple_of(((1 - low) * 2 + 1 - core) * (BLK // 4) + CHUNKS[-1][1], TILE)


def left_kernel(inverse, w_own, w_core, *refs):
    chunks, (out, weights) = refs[:-2], refs[-2:]
    _, y, core, _, _ = place()
    low = y % 2
    rows = w_core.shape[0]
    pieces = [(w_own.at[:, pl.ds(pl.multiple_of(core * BLK, BLK), BLK)], (low * 2 + core) * rows), (w_core, (low * 2 + 1 - core) * rows)]
    for chunk, (other, start, _) in zip(chunks, CHUNKS):
        lane = 1 - core if other else core
        pieces.append((chunk, ((1 - low) * 2 + lane) * rows + start))
    weights[pl.ds(last_start(low, core), CHUNKS[-1][2])] = jnp.zeros((CHUNKS[-1][2], BLK), jnp.bfloat16)
    for piece, there in pieces:
        weights[pl.ds(pl.multiple_of(there, 64), piece.shape[0])] = piece[...]
    for cols in steps():
        out[:, cols] = dot(inverse[...], weights[:, cols])


def right_kernel(
    first_own, first_got, second_own, second_got, part_left, inverse, chunk, theirs, mine, full, left, second, third
):
    x_hi, y, core, _, _ = place()
    code = x_hi * 4 + y
    rows = mine.shape[0]
    owns, gots = (first_own, second_own), (first_got, second_got)
    for tile, (i, j) in enumerate(UPPER):
        part, piece, at = slot_of(tile, code, WIDTH)
        index = (piece & 3) * (WIDTH, PIECE - WIDTH)[part] + at
        put(full, i, j, jnp.where(piece >= 4, gots[part][index], owns[part][index]))
    ratio, scale = scales(diagonal_sum(full))

    last = pl.ds(last_start(y % 2, core), CHUNKS[-1][2])
    for cols in steps():
        left[:, cols] = (part_left[:, cols] + dot(inverse[:, last], chunk[:, cols])).astype(jnp.bfloat16)

    def start_of(cols):
        turned = dot(left[...], full[:, cols])
        return 1.5 * left[:, cols].astype(jnp.float32) - 0.5 * ratio * turned

    def finish(cols, value):
        theirs[:, cols] = jnp.where(core == 0, value[rows:], value[:rows])
        mine[:, cols] = jnp.where(core == 0, value[:rows], value[rows:])

    newton_chain(full, ratio, scale, start_of, second, third, finish)


def whole(memory):
    return pl.BlockSpec(memory_space=memory)


def tiles(count):
    return jax.ShapeDtypeStruct((count, TILE, TILE), jnp.bfloat16)


def matrix(rows, cols):
    return pltpu.VMEM((rows, cols), jnp.bfloat16)


def shaped(rows, cols):
    return jax.ShapeDtypeStruct((rows, cols), jnp.bfloat16)


def kernel(body, name, operands, in_specs, out_shape, out_specs, scratch, flops, moved, vmem):
    return pl.pallas_call(
        body,
        out_shape=out_shape,
        in_specs=[whole(space) for space in in_specs],
        out_specs=jax.tree.map(whole, out_specs),
        scratch_shapes=scratch,
        compiler_params=pltpu.CompilerParams(vmem_limit_bytes=vmem * MIB),
        cost_estimate=pl.CostEstimate(flops=flops, bytes_accessed=moved, transcendentals=0),
        name=name,
    )(*operands)


def on_device(activations, out_grads, weight_grad):
    rows = weight_grad.shape[0]
    core = lax.axis_index("dp") % 2
    other = (1 - core) * BLK
    n, m, a = WIDTH, PIECE - WIDTH, A_PIECE

    g_other = lax.dynamic_slice_in_dim(out_grads, other, BLK, 1)
    w_0 = lax.dynamic_slice_in_dim(weight_grad, core * BLK, BLK, 1)
    g_other, w_0, activations = together(g_other, w_0, activations)
    g_got = send(g_other, CORE, "g_tokens")
    w_0 = send(w_0, Y_NEAR, "w_0")
    a_sent, a_kept, w_1, w_2, w_3 = kernel(
        cov_a,
        "cov_a",
        (activations, weight_grad),
        [pltpu.HBM, pltpu.HBM],
        [tiles(4 * a)] * 2 + [shaped(count, BLK) for _, _, count in CHUNKS[1:]],
        [pltpu.VMEM] * 2 + [pl.ANY] * (len(CHUNKS) - 1),
        [pltpu.VMEM((4, activations.shape[0], BLK), jnp.bfloat16), pltpu.SemaphoreType.DMA((3 + len(CHUNKS),))],
        40 * 2 * 256 * TILE * TILE,
        5 << 20,
        16,
    )
    a_swapped = send(a_sent, CORE, "a_core")

    a_swapped, g_got = together(a_swapped, g_got)
    a_sum = add(a_kept, a_swapped)
    a_parts = [a_sum[at * a : (at + 1) * a] for at in range(4)]
    a_both = send(a_parts[3], X_Y_FAR, "a_sum_both")
    a_x = send(a_parts[2], X_HALF, "a_sum_x")
    a_y = send(a_parts[1], Y_FAR, "a_sum_y")
    a_parts = [a_parts[0], a_y, a_x, a_both]
    first_send, second_send, first_keep, second_keep = kernel(
        cov_g,
        "cov_g",
        (out_grads, g_got),
        [pltpu.VMEM] * 2,
        [tiles(4 * n), tiles(4 * m), tiles(4 * n), tiles(4 * m)],
        [pltpu.VMEM] * 4,
        [matrix(2 * out_grads.shape[0], BLK)],
        21 * 2 * 512 * 256 * 256,
        4 << 20,
        16,
    )

    first_send, second_send, w_1, *a_parts = together(first_send, second_send, w_1, *a_parts)
    a_quarter = add(*a_parts)
    first_got = send(first_send, X_HALF, "sum_1_x")
    second_got = send(second_send, Y_FAR, "sum_1_y")
    a_near = send(a_quarter, Y_NEAR, "a_near")
    w_1 = send(w_1, Y_NEAR_CORE, "w_1")

    first_got, second_got, a_near, w_0, w_1 = together(first_got, second_got, a_near, w_0, w_1)
    first_next = send(add(first_keep[2 * n :], first_got[2 * n :]), Y_FAR, "sum_2_y")
    second_next = send(add(second_keep[2 * m :], second_got[2 * m :]), Y_NEAR, "sum_2_near")
    a_own = add(a_quarter, a_near)
    a_pair = send(a_own, X_NEAR, "a_pair")
    first_sum = add(first_keep[: 2 * n], first_got[: 2 * n])
    second_sum = add(second_keep[: 2 * m], second_got[: 2 * m])

    first_next, second_next, a_pair = together(first_next, second_next, a_pair)
    first_sum = add(first_sum, first_next)
    second_sum = add(second_sum, second_next)
    second_last = send(second_sum, X_HALF, "sum_3_x")
    first_last = send(first_sum, Y_NEAR, "sum_3_near")
    a_own = jnp.concatenate([a_own, a_pair])
    a_below, a_above = send(a_own, Z_UP, "a_up"), send(a_own, Z_DOWN, "a_down")

    first_last, second_last, w_2 = together(first_last, second_last, w_2)
    first_own = add(first_sum, swapped(first_last))
    second_own = add(second_sum, swapped(second_last))
    first_got = send(first_own, Y_FAR, "back_4_y")
    second_got = send(second_own, Y_NEAR, "back_4_near")
    a_far = [send(a_below[:a], Z_UP, "a_up_2"), send(a_above[a:], Z_DOWN, "a_down_2")]
    a_parts = (a_own, a_above, *a_far, a_below)
    a_swapped = [send(part, CORE, "a_core_back") for part in a_parts]
    w_core = send(lax.dynamic_slice_in_dim(weight_grad, other, BLK, 1), CORE, "w_core")
    w_2 = send(w_2, Y_NEAR_CORE, "w_2")

    first_got, second_got, w_core, w_2, w_3, a_own = together(first_got, second_got, w_core, w_2, w_3, a_own)
    first_own = jnp.concatenate([first_own, first_got])
    second_own = jnp.concatenate([second_own, second_got])
    first_got = send(first_own, X_HALF, "back_5_x")
    second_got = send(second_own, Y_FAR, "back_5_y")
    w_3 = send(w_3, Y_NEAR_CORE, "w_3")
    a_parts = (a_own, *a_parts[1:], *a_swapped)

    inverse = kernel(
        inverse_kernel,
        "inverse",
        a_parts,
        [pltpu.VMEM] * 10,
        shaped(2 * rows, BLK),
        pltpu.VMEM,
        [pltpu.VMEM((SLOTS, TILE, TILE), jnp.bfloat16), matrix(BLK, BLK), matrix(2 * rows, BLK), matrix(2 * rows, BLK)],
        4 * 2 * rows * BLK * BLK,
        5 << 20,
        24,
    )
    left = kernel(
        left_kernel,
        "left",
        (inverse, weight_grad, w_core, w_0, w_1, w_2),
        [pltpu.VMEM] * 6,
        jax.ShapeDtypeStruct((2 * rows, BLK), jnp.float32),
        pltpu.VMEM,
        [matrix(BLK, BLK)],
        2 * 2 * rows * BLK * BLK,
        9 << 20,
        20,
    )
    theirs, mine = kernel(
        right_kernel,
        "right",
        (first_own, first_got, second_own, second_got, left, inverse, w_3),
        [pltpu.VMEM] * 7,
        [shaped(rows, BLK)] * 2,
        [pltpu.VMEM] * 2,
        [matrix(BLK, BLK)] + [matrix(2 * rows, BLK)] * 3,
        6 * 2 * rows * BLK * BLK,
        8 << 20,
        24,
    )
    theirs = send(theirs, CORE, "out_core")
    out = jnp.zeros((rows, 2 * BLK), jnp.bfloat16)
    out = lax.dynamic_update_slice(out, mine, (0, core * BLK))
    return lax.dynamic_update_slice(out, theirs, (0, other))


def solution(mesh):
    return jax.shard_map(
        on_device,
        mesh=mesh,
        in_specs=(P("dp", None), P("dp", "tensor"), P("dp", "tensor")),
        out_specs=P("dp", "tensor"),
        check_vma=False,
    )
```

```python
import jax
import jax.numpy as jnp
from jax import lax
from jax.experimental import pallas as pl
from jax.experimental.pallas import tpu as pltpu
from jax.sharding import PartitionSpec as P

BLK = 1536
TOKENS = 4096
TILE = 128
SIDE = BLK // TILE
UPPER = [(i, j) for i in range(SIDE) for j in range(i, SIDE)]
SLOTS = 80
PIECE = 10
WIDTH = 5
A_PIECE = 5
STEP = 256
CHUNKS = ((0, 0, 384), (1, 0, 64), (1, 64, 64), (1, 128, 256))
AXES = ("dp", "tensor")
MIB = 1024 * 1024


def moves(target):
    pairs = []
    for dp in range(16):
        for tp in range(8):
            x_hi, y, core = dp // 8, dp // 2 % 4, dp % 2
            x_lo, z = tp // 4, tp % 4
            x_hi, y, core, x_lo, z = target(x_hi, y, core, x_lo, z)
            there = (x_hi * 8 + y * 2 + core) * 8 + x_lo * 4 + z % 4
            pairs.append((dp * 8 + tp, there))
    return pairs


CORE = moves(lambda h, y, c, l, z: (h, y, c ^ 1, l, z))
Y_NEAR = moves(lambda h, y, c, l, z: (h, y ^ 1, c, l, z))
Y_NEAR_CORE = moves(lambda h, y, c, l, z: (h, y ^ 1, c ^ 1, l, z))
Y_FAR = moves(lambda h, y, c, l, z: (h, y ^ 3, c, l, z))
X_HALF = moves(lambda h, y, c, l, z: (h ^ 1, y, c, l, z))
X_Y_FAR = moves(lambda h, y, c, l, z: (h ^ 1, y ^ 3, c, l, z))
X_NEAR = moves(lambda h, y, c, l, z: (h, y, c, l ^ 1, z))
Z_UP = moves(lambda h, y, c, l, z: (h, y, c, l, z + 1))
Z_DOWN = moves(lambda h, y, c, l, z: (h, y, c, l, z + 3))
Z_HALF = moves(lambda h, y, c, l, z: (h, y, c, l, z + 2))


def send(array, pairs, name):
    with jax.named_scope(name):
        return lax.ppermute(array, AXES, pairs)


def together(*values):
    return lax.optimization_barrier(values)


def add(*terms):
    return sum(term.astype(jnp.float32) for term in terms).astype(jnp.bfloat16)


def swapped(array):
    half = array.shape[0] // 2
    return jnp.concatenate([array[half:], array[:half]])


def place():
    dp, tp = lax.axis_index("dp"), lax.axis_index("tensor")
    return dp // 8, dp // 2 % 4, dp % 2, tp // 4, tp % 4


def slot_first(piece, code):
    rel = piece ^ code
    return rel ^ (rel >> 1 & 1)


def slot_second(piece, code):
    rel = piece ^ code
    low, mid, high = rel & 1, rel >> 1 & 1, rel >> 2
    return mid << 2 | (low ^ mid) << 1 | high


def slot_of(tile, code, width):
    piece, at = tile // PIECE, tile % PIECE
    if at < width:
        return 0, slot_first(piece, code), at
    return 1, slot_second(piece, code), at - width


def cov_g(own, got, first_send, second_send, first_keep, second_keep, tokens):
    x_hi, y, core, _, _ = place()
    half = own.shape[0]
    tokens[:half] = own[:, pl.ds(pl.multiple_of(core * BLK, BLK), BLK)]
    tokens[half:] = got[...]
    code = x_hi * 4 + y
    sends, keeps = (first_send, second_send), (first_keep, second_keep)

    def store(tile, value):
        part, piece, at = slot_of(tile, code, WIDTH)
        count = (WIDTH, PIECE - WIDTH)[part]

        @pl.when(piece >= 4)
        def _():
            sends[part][(piece - 4) * count + at] = value

        @pl.when(piece < 4)
        def _():
            keeps[part][piece * count + at] = value

    for row in range(SIDE // 2):
        start = row * 2 * TILE
        product = lax.dot_general(
            tokens[:, start : start + 2 * TILE],
            tokens[:, start:],
            (((0,), (0,)), ((), ())),
            preferred_element_type=jnp.float32,
        ).astype(jnp.bfloat16)
        for tile, (i, j) in enumerate(UPPER):
            if i // 2 == row:
                top, left = (i - 2 * row) * TILE, (j - 2 * row) * TILE
                store(tile, product[top : top + TILE, left : left + TILE])
    for tile in range(len(UPPER), SLOTS):
        store(tile, jnp.zeros((TILE, TILE), jnp.bfloat16))


def corner(tile):
    starts = [i * SIDE - i * (i - 1) // 2 for i in range(SIDE)]
    i = sum((tile >= start).astype(jnp.int32) for start in starts[1:])
    return i, jnp.minimum(tile - (i * SIDE - i * (i - 1) // 2) + i, SIDE - 1)


def cov_a(whole_tokens, whole_weights, sent, kept, *refs):
    chunks, (tokens, sems) = refs[:-2], refs[-2:]
    x_hi, y, core, x_lo, z = place()
    tp = x_lo * 4 + z
    own = x_hi * 2 + y // 2
    loads = [
        pltpu.make_async_copy(
            whole_tokens.at[:, pl.ds(pl.multiple_of((own ^ rel) * BLK, BLK), BLK)], tokens.at[rel], sems.at[rel]
        )
        for rel in range(4)
    ]
    cuts = [
        pltpu.make_async_copy(
            whole_weights.at[pl.ds(start, count), pl.ds(pl.multiple_of((core ^ lane) * BLK, BLK), BLK)],
            chunk,
            sems.at[4 + at],
        )
        for at, ((lane, start, count), chunk) in enumerate(zip(CHUNKS[1:], chunks))
    ]
    for copy in loads + cuts:
        copy.start()
    for rel, load in enumerate(loads):
        load.wait()
        for out, side in ((sent, 1 - core), (kept, core)):
            for at in range(A_PIECE):
                i, j = corner((tp * 2 + side) * A_PIECE + at)
                left, right = (
                    tokens[rel, :, pl.ds(pl.multiple_of(place_of * TILE, TILE), TILE)] for place_of in (i, j)
                )
                out[rel * A_PIECE + at] = lax.dot_general(
                    left, right, (((0,), (0,)), ((), ())), preferred_element_type=jnp.float32
                ).astype(jnp.bfloat16)
    for copy in cuts:
        copy.wait()


def put(full, i, j, value):
    full[i * TILE : (i + 1) * TILE, j * TILE : (j + 1) * TILE] = value
    if i != j:
        full[j * TILE : (j + 1) * TILE, i * TILE : (i + 1) * TILE] = value.T


def diagonal_sum(full):
    row = lax.broadcasted_iota(jnp.int32, (TILE, TILE), 0)
    col = lax.broadcasted_iota(jnp.int32, (TILE, TILE), 1)
    total = jnp.zeros((TILE, TILE), jnp.float32)
    for at in range(0, BLK, TILE):
        total = total + full[at : at + TILE, at : at + TILE].astype(jnp.float32)
    return jnp.sum(jnp.where(row == col, total, 0.0))


def scales(trace):
    mean = trace / (TOKENS * BLK) + 1e-06
    return 1.0 / (TOKENS * mean), 1.0 / (2.0 * mean)


def steps():
    return [slice(at, at + STEP) for at in range(0, BLK, STEP)]


def dot(left, right):
    return jnp.dot(left, right, preferred_element_type=jnp.float32)


def newton_chain(full, ratio, scale, start_of, second, third, finish):
    for cols in steps():
        second[:, cols] = start_of(cols).astype(jnp.bfloat16)
    for cols in steps():
        turned = dot(second[...], full[:, cols])
        third[:, cols] = (second[:, cols].astype(jnp.float32) + ratio * turned).astype(jnp.bfloat16)
    for cols in steps():
        turned = dot(third[...], full[:, cols])
        value = 2.0 * second[:, cols].astype(jnp.float32) - 0.75 * third[:, cols].astype(jnp.float32)
        finish(cols, (scale * (value + 0.25 * ratio * turned)).astype(jnp.bfloat16))


def inverse_kernel(*refs):
    parts, out, packed, full, second, third = refs[:10], *refs[10:]
    _, y, core, x_lo, z = place()
    rows = out.shape[0]
    start = 0
    for part in parts:
        packed[start : start + part.shape[0]] = part[...]
        start += part.shape[0]
    for tile, (i, j) in enumerate(UPPER):
        piece, at = tile // A_PIECE, tile % A_PIECE
        side, z_at, x_at = piece % 2, piece // 2 % 4, piece // 8
        slot = (((side ^ core) * 4 + (z_at - z + 4) % 4) * 2 + (x_at ^ x_lo)) * A_PIECE + at
        put(full, i, j, packed[slot])
    ratio, scale = scales(diagonal_sum(full))
    first_row = pl.multiple_of(y % 2 * rows, rows)

    def start_of(cols):
        row = lax.broadcasted_iota(jnp.int32, (rows, STEP), 0) + first_row
        col = lax.broadcasted_iota(jnp.int32, (rows, STEP), 1) + cols.start
        return jnp.where(row == col, 1.5, 0.0) - 0.5 * ratio * full[pl.ds(first_row, rows), cols].astype(jnp.float32)

    def finish(cols, value):
        out[:, cols] = value

    newton_chain(full, ratio, scale, start_of, second, third, finish)


def last_start(low, core):
    return pl.multiple_of(((1 - low) * 2 + 1 - core) * (BLK // 4) + CHUNKS[-1][1], TILE)


def left_kernel(inverse, w_own, w_core, *refs):
    chunks, (out, weights) = refs[:-2], refs[-2:]
    _, y, core, _, _ = place()
    low = y % 2
    rows = w_core.shape[0]
    pieces = [(w_own.at[:, pl.ds(pl.multiple_of(core * BLK, BLK), BLK)], (low * 2 + core) * rows), (w_core, (low * 2 + 1 - core) * rows)]
    for chunk, (other, start, _) in zip(chunks, CHUNKS):
        lane = 1 - core if other else core
        pieces.append((chunk, ((1 - low) * 2 + lane) * rows + start))
    weights[pl.ds(last_start(low, core), CHUNKS[-1][2])] = jnp.zeros((CHUNKS[-1][2], BLK), jnp.bfloat16)
    for piece, there in pieces:
        weights[pl.ds(pl.multiple_of(there, 64), piece.shape[0])] = piece[...]
    for cols in steps():
        out[:, cols] = dot(inverse[...], weights[:, cols])


def right_kernel(
    first_own, first_got, second_own, second_got, part_left, inverse, chunk, theirs, mine, full, left, second, third
):
    x_hi, y, core, _, _ = place()
    code = x_hi * 4 + y
    rows = mine.shape[0]
    owns, gots = (first_own, second_own), (first_got, second_got)
    for tile, (i, j) in enumerate(UPPER):
        part, piece, at = slot_of(tile, code, WIDTH)
        index = (piece & 3) * (WIDTH, PIECE - WIDTH)[part] + at
        put(full, i, j, jnp.where(piece >= 4, gots[part][index], owns[part][index]))
    ratio, scale = scales(diagonal_sum(full))

    last = pl.ds(last_start(y % 2, core), CHUNKS[-1][2])
    for cols in steps():
        left[:, cols] = (part_left[:, cols] + dot(inverse[:, last], chunk[:, cols])).astype(jnp.bfloat16)

    def start_of(cols):
        turned = dot(left[...], full[:, cols])
        return 1.5 * left[:, cols].astype(jnp.float32) - 0.5 * ratio * turned

    def finish(cols, value):
        theirs[:, cols] = jnp.where(core == 0, value[rows:], value[:rows])
        mine[:, cols] = jnp.where(core == 0, value[:rows], value[rows:])

    newton_chain(full, ratio, scale, start_of, second, third, finish)


def whole(memory):
    return pl.BlockSpec(memory_space=memory)


def tiles(count):
    return jax.ShapeDtypeStruct((count, TILE, TILE), jnp.bfloat16)


def matrix(rows, cols):
    return pltpu.VMEM((rows, cols), jnp.bfloat16)


def shaped(rows, cols):
    return jax.ShapeDtypeStruct((rows, cols), jnp.bfloat16)


def kernel(body, name, operands, in_specs, out_shape, out_specs, scratch, flops, moved, vmem):
    return pl.pallas_call(
        body,
        out_shape=out_shape,
        in_specs=[whole(space) for space in in_specs],
        out_specs=jax.tree.map(whole, out_specs),
        scratch_shapes=scratch,
        compiler_params=pltpu.CompilerParams(vmem_limit_bytes=vmem * MIB),
        cost_estimate=pl.CostEstimate(flops=flops, bytes_accessed=moved, transcendentals=0),
        name=name,
    )(*operands)


def on_device(activations, out_grads, weight_grad):
    rows = weight_grad.shape[0]
    core = lax.axis_index("dp") % 2
    other = (1 - core) * BLK
    n, m, a = WIDTH, PIECE - WIDTH, A_PIECE

    g_other = lax.dynamic_slice_in_dim(out_grads, other, BLK, 1)
    w_0 = lax.dynamic_slice_in_dim(weight_grad, core * BLK, BLK, 1)
    g_other, w_0, activations = together(g_other, w_0, activations)
    g_got = send(g_other, CORE, "g_tokens")
    w_0 = send(w_0, Y_NEAR, "w_0")
    a_sent, a_kept, w_1, w_2, w_3 = kernel(
        cov_a,
        "cov_a",
        (activations, weight_grad),
        [pltpu.HBM, pltpu.HBM],
        [tiles(4 * a)] * 2 + [shaped(count, BLK) for _, _, count in CHUNKS[1:]],
        [pltpu.VMEM] * 2 + [pl.ANY] * (len(CHUNKS) - 1),
        [pltpu.VMEM((4, activations.shape[0], BLK), jnp.bfloat16), pltpu.SemaphoreType.DMA((3 + len(CHUNKS),))],
        40 * 2 * 256 * TILE * TILE,
        5 << 20,
        16,
    )
    a_swapped = send(a_sent, CORE, "a_core")

    a_swapped, g_got = together(a_swapped, g_got)
    a_sum = add(a_kept, a_swapped)
    a_parts = [a_sum[at * a : (at + 1) * a] for at in range(4)]
    a_both = send(a_parts[3], X_Y_FAR, "a_sum_both")
    a_x = send(a_parts[2], X_HALF, "a_sum_x")
    a_y = send(a_parts[1], Y_FAR, "a_sum_y")
    a_parts = [a_parts[0], a_y, a_x, a_both]
    first_send, second_send, first_keep, second_keep = kernel(
        cov_g,
        "cov_g",
        (out_grads, g_got),
        [pltpu.VMEM] * 2,
        [tiles(4 * n), tiles(4 * m), tiles(4 * n), tiles(4 * m)],
        [pltpu.VMEM] * 4,
        [matrix(2 * out_grads.shape[0], BLK)],
        21 * 2 * 512 * 256 * 256,
        4 << 20,
        16,
    )

    first_send, second_send, w_1, *a_parts = together(first_send, second_send, w_1, *a_parts)
    a_quarter = add(*a_parts)
    first_got = send(first_send, X_HALF, "sum_1_x")
    second_got = send(second_send, Y_FAR, "sum_1_y")
    a_near = send(a_quarter, Y_NEAR, "a_near")
    w_1 = send(w_1, Y_NEAR_CORE, "w_1")

    first_got, second_got, a_near, w_0, w_1 = together(first_got, second_got, a_near, w_0, w_1)
    first_next = send(add(first_keep[2 * n :], first_got[2 * n :]), Y_FAR, "sum_2_y")
    second_next = send(add(second_keep[2 * m :], second_got[2 * m :]), Y_NEAR, "sum_2_near")
    a_own = add(a_quarter, a_near)
    a_pair = send(a_own, X_NEAR, "a_pair")
    first_sum = add(first_keep[: 2 * n], first_got[: 2 * n])
    second_sum = add(second_keep[: 2 * m], second_got[: 2 * m])

    first_next, second_next, a_pair = together(first_next, second_next, a_pair)
    first_sum = add(first_sum, first_next)
    second_sum = add(second_sum, second_next)
    second_last = send(second_sum, X_HALF, "sum_3_x")
    first_last = send(first_sum, Y_NEAR, "sum_3_near")
    a_own = jnp.concatenate([a_own, a_pair])
    a_below, a_above = send(a_own, Z_UP, "a_up"), send(a_own, Z_DOWN, "a_down")

    first_last, second_last, w_2 = together(first_last, second_last, w_2)
    first_own = add(first_sum, swapped(first_last))
    second_own = add(second_sum, swapped(second_last))
    first_got = send(first_own, Y_FAR, "back_4_y")
    second_got = send(second_own, Y_NEAR, "back_4_near")
    a_far = [send(a_below[:a], Z_UP, "a_up_2"), send(a_above[a:], Z_DOWN, "a_down_2")]
    a_parts = (a_own, a_above, *a_far, a_below)
    w_core = send(lax.dynamic_slice_in_dim(weight_grad, other, BLK, 1), CORE, "w_core")
    w_2 = send(w_2, Y_NEAR_CORE, "w_2")

    first_got, second_got, w_core, w_2, w_3, *a_parts = together(first_got, second_got, w_core, w_2, w_3, *a_parts)
    first_own = jnp.concatenate([first_own, first_got])
    second_own = jnp.concatenate([second_own, second_got])
    first_got = send(first_own, X_HALF, "back_5_x")
    second_got = send(second_own, Y_FAR, "back_5_y")
    w_3 = send(w_3, Y_NEAR_CORE, "w_3")
    a_parts = (*a_parts, *(send(part, CORE, "a_core_back") for part in a_parts))

    inverse = kernel(
        inverse_kernel,
        "inverse",
        a_parts,
        [pltpu.VMEM] * 10,
        shaped(2 * rows, BLK),
        pltpu.VMEM,
        [pltpu.VMEM((SLOTS, TILE, TILE), jnp.bfloat16), matrix(BLK, BLK), matrix(2 * rows, BLK), matrix(2 * rows, BLK)],
        4 * 2 * rows * BLK * BLK,
        5 << 20,
        24,
    )
    left = kernel(
        left_kernel,
        "left",
        (inverse, weight_grad, w_core, w_0, w_1, w_2),
        [pltpu.VMEM] * 6,
        jax.ShapeDtypeStruct((2 * rows, BLK), jnp.float32),
        pltpu.VMEM,
        [matrix(BLK, BLK)],
        2 * 2 * rows * BLK * BLK,
        9 << 20,
        20,
    )
    theirs, mine = kernel(
        right_kernel,
        "right",
        (first_own, first_got, second_own, second_got, left, inverse, w_3),
        [pltpu.VMEM] * 7,
        [shaped(rows, BLK)] * 2,
        [pltpu.VMEM] * 2,
        [matrix(BLK, BLK)] + [matrix(2 * rows, BLK)] * 3,
        6 * 2 * rows * BLK * BLK,
        8 << 20,
        24,
    )
    theirs = send(theirs, CORE, "out_core")
    out = jnp.zeros((rows, 2 * BLK), jnp.bfloat16)
    out = lax.dynamic_update_slice(out, mine, (0, core * BLK))
    return lax.dynamic_update_slice(out, theirs, (0, other))


def solution(mesh):
    return jax.shard_map(
        on_device,
        mesh=mesh,
        in_specs=(P("dp", None), P("dp", "tensor"), P("dp", "tensor")),
        out_specs=P("dp", "tensor"),
        check_vma=False,
    )
```

```python
import jax
import jax.numpy as jnp
from jax import lax
from jax.experimental import pallas as pl
from jax.experimental.pallas import tpu as pltpu
from jax.sharding import PartitionSpec as P

BLK = 1536
TOKENS = 4096
TILE = 128
SIDE = BLK // TILE
UPPER = [(i, j) for i in range(SIDE) for j in range(i, SIDE)]
SLOTS = 80
PIECE = 10
WIDTH = 5
A_PIECE = 5
STEP = 256
CHUNKS = ((0, 0, 384), (1, 0, 64), (1, 64, 64), (1, 128, 256))
AXES = ("dp", "tensor")
MIB = 1024 * 1024


def moves(target):
    pairs = []
    for dp in range(16):
        for tp in range(8):
            x_hi, y, core = dp // 8, dp // 2 % 4, dp % 2
            x_lo, z = tp // 4, tp % 4
            x_hi, y, core, x_lo, z = target(x_hi, y, core, x_lo, z)
            there = (x_hi * 8 + y * 2 + core) * 8 + x_lo * 4 + z % 4
            pairs.append((dp * 8 + tp, there))
    return pairs


CORE = moves(lambda h, y, c, l, z: (h, y, c ^ 1, l, z))
Y_NEAR = moves(lambda h, y, c, l, z: (h, y ^ 1, c, l, z))
Y_NEAR_CORE = moves(lambda h, y, c, l, z: (h, y ^ 1, c ^ 1, l, z))
Y_FAR = moves(lambda h, y, c, l, z: (h, y ^ 3, c, l, z))
X_HALF = moves(lambda h, y, c, l, z: (h ^ 1, y, c, l, z))
X_Y_FAR = moves(lambda h, y, c, l, z: (h ^ 1, y ^ 3, c, l, z))
X_NEAR = moves(lambda h, y, c, l, z: (h, y, c, l ^ 1, z))
Z_UP = moves(lambda h, y, c, l, z: (h, y, c, l, z + 1))
Z_DOWN = moves(lambda h, y, c, l, z: (h, y, c, l, z + 3))
Z_HALF = moves(lambda h, y, c, l, z: (h, y, c, l, z + 2))


def send(array, pairs, name):
    with jax.named_scope(name):
        return lax.ppermute(array, AXES, pairs)


def together(*values):
    return lax.optimization_barrier(values)


def add(*terms):
    return sum(term.astype(jnp.float32) for term in terms).astype(jnp.bfloat16)


def swapped(array):
    half = array.shape[0] // 2
    return jnp.concatenate([array[half:], array[:half]])


def place():
    dp, tp = lax.axis_index("dp"), lax.axis_index("tensor")
    return dp // 8, dp // 2 % 4, dp % 2, tp // 4, tp % 4


def slot_first(piece, code):
    rel = piece ^ code
    return rel ^ (rel >> 1 & 1)


def slot_second(piece, code):
    rel = piece ^ code
    low, mid, high = rel & 1, rel >> 1 & 1, rel >> 2
    return mid << 2 | (low ^ mid) << 1 | high


def slot_of(tile, code, width):
    piece, at = tile // PIECE, tile % PIECE
    if at < width:
        return 0, slot_first(piece, code), at
    return 1, slot_second(piece, code), at - width


def cov_g(own, got, first_send, second_send, first_keep, second_keep, tokens):
    x_hi, y, core, _, _ = place()
    half = own.shape[0]
    tokens[:half] = own[:, pl.ds(pl.multiple_of(core * BLK, BLK), BLK)]
    tokens[half:] = got[...]
    code = x_hi * 4 + y
    sends, keeps = (first_send, second_send), (first_keep, second_keep)

    def store(tile, value):
        part, piece, at = slot_of(tile, code, WIDTH)
        count = (WIDTH, PIECE - WIDTH)[part]

        @pl.when(piece >= 4)
        def _():
            sends[part][(piece - 4) * count + at] = value

        @pl.when(piece < 4)
        def _():
            keeps[part][piece * count + at] = value

    for row in range(SIDE // 2):
        start = row * 2 * TILE
        product = lax.dot_general(
            tokens[:, start : start + 2 * TILE],
            tokens[:, start:],
            (((0,), (0,)), ((), ())),
            preferred_element_type=jnp.float32,
        ).astype(jnp.bfloat16)
        for tile, (i, j) in enumerate(UPPER):
            if i // 2 == row:
                top, left = (i - 2 * row) * TILE, (j - 2 * row) * TILE
                store(tile, product[top : top + TILE, left : left + TILE])
    for tile in range(len(UPPER), SLOTS):
        store(tile, jnp.zeros((TILE, TILE), jnp.bfloat16))


def corner(tile):
    starts = [i * SIDE - i * (i - 1) // 2 for i in range(SIDE)]
    i = sum((tile >= start).astype(jnp.int32) for start in starts[1:])
    return i, jnp.minimum(tile - (i * SIDE - i * (i - 1) // 2) + i, SIDE - 1)


def cov_a(whole_tokens, whole_weights, sent, kept, *refs):
    chunks, (tokens, sems) = refs[:-2], refs[-2:]
    x_hi, y, core, x_lo, z = place()
    tp = x_lo * 4 + z
    own = x_hi * 2 + y // 2
    loads = [
        pltpu.make_async_copy(
            whole_tokens.at[:, pl.ds(pl.multiple_of((own ^ rel) * BLK, BLK), BLK)], tokens.at[rel], sems.at[rel]
        )
        for rel in range(4)
    ]
    cuts = [
        pltpu.make_async_copy(
            whole_weights.at[pl.ds(start, count), pl.ds(pl.multiple_of((core ^ lane) * BLK, BLK), BLK)],
            chunk,
            sems.at[4 + at],
        )
        for at, ((lane, start, count), chunk) in enumerate(zip(CHUNKS[1:], chunks))
    ]
    for copy in loads + cuts:
        copy.start()
    for rel, load in enumerate(loads):
        load.wait()
        for out, side in ((sent, 1 - core), (kept, core)):
            for at in range(A_PIECE):
                i, j = corner((tp * 2 + side) * A_PIECE + at)
                left, right = (
                    tokens[rel, :, pl.ds(pl.multiple_of(place_of * TILE, TILE), TILE)] for place_of in (i, j)
                )
                out[rel * A_PIECE + at] = lax.dot_general(
                    left, right, (((0,), (0,)), ((), ())), preferred_element_type=jnp.float32
                ).astype(jnp.bfloat16)
    for copy in cuts:
        copy.wait()


def put(full, i, j, value):
    full[i * TILE : (i + 1) * TILE, j * TILE : (j + 1) * TILE] = value
    if i != j:
        full[j * TILE : (j + 1) * TILE, i * TILE : (i + 1) * TILE] = value.T


def diagonal_sum(full):
    row = lax.broadcasted_iota(jnp.int32, (TILE, TILE), 0)
    col = lax.broadcasted_iota(jnp.int32, (TILE, TILE), 1)
    total = jnp.zeros((TILE, TILE), jnp.float32)
    for at in range(0, BLK, TILE):
        total = total + full[at : at + TILE, at : at + TILE].astype(jnp.float32)
    return jnp.sum(jnp.where(row == col, total, 0.0))


def scales(trace):
    mean = trace / (TOKENS * BLK) + 1e-06
    return 1.0 / (TOKENS * mean), 1.0 / (2.0 * mean)


def steps():
    return [slice(at, at + STEP) for at in range(0, BLK, STEP)]


def dot(left, right):
    return jnp.dot(left, right, preferred_element_type=jnp.float32)


def newton_chain(full, ratio, scale, start_of, second, third, finish):
    for cols in steps():
        second[:, cols] = start_of(cols).astype(jnp.bfloat16)
    for cols in steps():
        turned = dot(second[...], full[:, cols])
        third[:, cols] = (second[:, cols].astype(jnp.float32) + ratio * turned).astype(jnp.bfloat16)
    for cols in steps():
        turned = dot(third[...], full[:, cols])
        value = 2.0 * second[:, cols].astype(jnp.float32) - 0.75 * third[:, cols].astype(jnp.float32)
        finish(cols, (scale * (value + 0.25 * ratio * turned)).astype(jnp.bfloat16))


def inverse_kernel(*refs):
    parts, out, packed, full, second, third = refs[:10], *refs[10:]
    _, y, core, x_lo, z = place()
    rows = out.shape[0]
    start = 0
    for part in parts:
        packed[start : start + part.shape[0]] = part[...]
        start += part.shape[0]
    for tile, (i, j) in enumerate(UPPER):
        piece, at = tile // A_PIECE, tile % A_PIECE
        side, z_at, x_at = piece % 2, piece // 2 % 4, piece // 8
        slot = (((side ^ core) * 4 + (z_at - z + 4) % 4) * 2 + (x_at ^ x_lo)) * A_PIECE + at
        put(full, i, j, packed[slot])
    ratio, scale = scales(diagonal_sum(full))
    first_row = pl.multiple_of(y % 2 * rows, rows)

    def start_of(cols):
        row = lax.broadcasted_iota(jnp.int32, (rows, STEP), 0) + first_row
        col = lax.broadcasted_iota(jnp.int32, (rows, STEP), 1) + cols.start
        return jnp.where(row == col, 1.5, 0.0) - 0.5 * ratio * full[pl.ds(first_row, rows), cols].astype(jnp.float32)

    def finish(cols, value):
        out[:, cols] = value

    newton_chain(full, ratio, scale, start_of, second, third, finish)


def last_start(low, core):
    return pl.multiple_of(((1 - low) * 2 + 1 - core) * (BLK // 4) + CHUNKS[-1][1], TILE)


def left_kernel(inverse, w_own, w_core, *refs):
    chunks, (out, weights) = refs[:-2], refs[-2:]
    _, y, core, _, _ = place()
    low = y % 2
    rows = w_core.shape[0]
    pieces = [(w_own.at[:, pl.ds(pl.multiple_of(core * BLK, BLK), BLK)], (low * 2 + core) * rows), (w_core, (low * 2 + 1 - core) * rows)]
    for chunk, (other, start, _) in zip(chunks, CHUNKS):
        lane = 1 - core if other else core
        pieces.append((chunk, ((1 - low) * 2 + lane) * rows + start))
    weights[pl.ds(last_start(low, core), CHUNKS[-1][2])] = jnp.zeros((CHUNKS[-1][2], BLK), jnp.bfloat16)
    for piece, there in pieces:
        weights[pl.ds(pl.multiple_of(there, 64), piece.shape[0])] = piece[...]
    for cols in steps():
        out[:, cols] = dot(inverse[...], weights[:, cols])


def spread_kernel(first_own, first_got, second_own, second_got, full):
    x_hi, y, _, _, _ = place()
    code = x_hi * 4 + y
    owns, gots = (first_own, second_own), (first_got, second_got)
    for tile, (i, j) in enumerate(UPPER):
        part, piece, at = slot_of(tile, code, WIDTH)
        index = (piece & 3) * (WIDTH, PIECE - WIDTH)[part] + at
        put(full, i, j, jnp.where(piece >= 4, gots[part][index], owns[part][index]))


def right_kernel(full, part_left, inverse, chunk, theirs, mine, left, second, third):
    _, y, core, _, _ = place()
    rows = mine.shape[0]
    ratio, scale = scales(diagonal_sum(full))
    last = pl.ds(last_start(y % 2, core), CHUNKS[-1][2])
    for cols in steps():
        left[:, cols] = (part_left[:, cols] + dot(inverse[:, last], chunk[:, cols])).astype(jnp.bfloat16)

    def start_of(cols):
        turned = dot(left[...], full[:, cols])
        return 1.5 * left[:, cols].astype(jnp.float32) - 0.5 * ratio * turned

    def finish(cols, value):
        theirs[:, cols] = jnp.where(core == 0, value[rows:], value[:rows])
        mine[:, cols] = jnp.where(core == 0, value[:rows], value[rows:])

    newton_chain(full, ratio, scale, start_of, second, third, finish)


def whole(memory):
    return pl.BlockSpec(memory_space=memory)


def tiles(count):
    return jax.ShapeDtypeStruct((count, TILE, TILE), jnp.bfloat16)


def matrix(rows, cols):
    return pltpu.VMEM((rows, cols), jnp.bfloat16)


def shaped(rows, cols):
    return jax.ShapeDtypeStruct((rows, cols), jnp.bfloat16)


def kernel(body, name, operands, in_specs, out_shape, out_specs, scratch, flops, moved, vmem):
    return pl.pallas_call(
        body,
        out_shape=out_shape,
        in_specs=[whole(space) for space in in_specs],
        out_specs=jax.tree.map(whole, out_specs),
        scratch_shapes=scratch,
        compiler_params=pltpu.CompilerParams(vmem_limit_bytes=vmem * MIB),
        cost_estimate=pl.CostEstimate(flops=flops, bytes_accessed=moved, transcendentals=0),
        name=name,
    )(*operands)


def on_device(activations, out_grads, weight_grad):
    rows = weight_grad.shape[0]
    core = lax.axis_index("dp") % 2
    other = (1 - core) * BLK
    n, m, a = WIDTH, PIECE - WIDTH, A_PIECE

    g_other = lax.dynamic_slice_in_dim(out_grads, other, BLK, 1)
    w_0 = lax.dynamic_slice_in_dim(weight_grad, core * BLK, BLK, 1)
    g_other, w_0, activations = together(g_other, w_0, activations)
    g_got = send(g_other, CORE, "g_tokens")
    w_0 = send(w_0, Y_NEAR, "w_0")
    a_sent, a_kept, w_1, w_2, w_3 = kernel(
        cov_a,
        "cov_a",
        (activations, weight_grad),
        [pltpu.HBM, pltpu.HBM],
        [tiles(4 * a)] * 2 + [shaped(count, BLK) for _, _, count in CHUNKS[1:]],
        [pltpu.VMEM] * 2 + [pl.ANY] * (len(CHUNKS) - 1),
        [pltpu.VMEM((4, activations.shape[0], BLK), jnp.bfloat16), pltpu.SemaphoreType.DMA((3 + len(CHUNKS),))],
        40 * 2 * 256 * TILE * TILE,
        5 << 20,
        16,
    )
    a_swapped = send(a_sent, CORE, "a_core")

    a_swapped, g_got = together(a_swapped, g_got)
    a_sum = add(a_kept, a_swapped)
    a_parts = [a_sum[at * a : (at + 1) * a] for at in range(4)]
    a_both = send(a_parts[3], X_Y_FAR, "a_sum_both")
    a_x = send(a_parts[2], X_HALF, "a_sum_x")
    a_y = send(a_parts[1], Y_FAR, "a_sum_y")
    a_parts = [a_parts[0], a_y, a_x, a_both]
    first_send, second_send, first_keep, second_keep = kernel(
        cov_g,
        "cov_g",
        (out_grads, g_got),
        [pltpu.VMEM] * 2,
        [tiles(4 * n), tiles(4 * m), tiles(4 * n), tiles(4 * m)],
        [pltpu.VMEM] * 4,
        [matrix(2 * out_grads.shape[0], BLK)],
        21 * 2 * 512 * 256 * 256,
        4 << 20,
        16,
    )

    first_send, second_send, w_1, *a_parts = together(first_send, second_send, w_1, *a_parts)
    a_quarter = add(*a_parts)
    first_got = send(first_send, X_HALF, "sum_1_x")
    second_got = send(second_send, Y_FAR, "sum_1_y")
    a_near = send(a_quarter, Y_NEAR, "a_near")
    w_1 = send(w_1, Y_NEAR_CORE, "w_1")

    first_got, second_got, a_near, w_0, w_1 = together(first_got, second_got, a_near, w_0, w_1)
    first_next = send(add(first_keep[2 * n :], first_got[2 * n :]), Y_FAR, "sum_2_y")
    second_next = send(add(second_keep[2 * m :], second_got[2 * m :]), Y_NEAR, "sum_2_near")
    a_own = add(a_quarter, a_near)
    a_pair = send(a_own, X_NEAR, "a_pair")
    first_sum = add(first_keep[: 2 * n], first_got[: 2 * n])
    second_sum = add(second_keep[: 2 * m], second_got[: 2 * m])

    first_next, second_next, a_pair = together(first_next, second_next, a_pair)
    first_sum = add(first_sum, first_next)
    second_sum = add(second_sum, second_next)
    second_last = send(second_sum, X_HALF, "sum_3_x")
    first_last = send(first_sum, Y_NEAR, "sum_3_near")
    a_own = jnp.concatenate([a_own, a_pair])
    a_below, a_above = send(a_own, Z_UP, "a_up"), send(a_own, Z_DOWN, "a_down")

    first_last, second_last, w_2 = together(first_last, second_last, w_2)
    first_own = add(first_sum, swapped(first_last))
    second_own = add(second_sum, swapped(second_last))
    first_got = send(first_own, Y_FAR, "back_4_y")
    second_got = send(second_own, Y_NEAR, "back_4_near")
    a_far = [send(a_below[:a], Z_UP, "a_up_2"), send(a_above[a:], Z_DOWN, "a_down_2")]
    a_parts = (a_own, a_above, *a_far, a_below)
    a_swapped = [send(part, CORE, "a_core_back") for part in a_parts]
    w_core = send(lax.dynamic_slice_in_dim(weight_grad, other, BLK, 1), CORE, "w_core")
    w_2 = send(w_2, Y_NEAR_CORE, "w_2")

    first_got, second_got, w_core, w_2, w_3, a_own = together(first_got, second_got, w_core, w_2, w_3, a_own)
    first_own = jnp.concatenate([first_own, first_got])
    second_own = jnp.concatenate([second_own, second_got])
    first_got = send(first_own, X_HALF, "back_5_x")
    second_got = send(second_own, Y_FAR, "back_5_y")
    w_3 = send(w_3, Y_NEAR_CORE, "w_3")
    a_parts = (a_own, *a_parts[1:], *a_swapped)

    inverse = kernel(
        inverse_kernel,
        "inverse",
        a_parts,
        [pltpu.VMEM] * 10,
        shaped(2 * rows, BLK),
        pltpu.VMEM,
        [pltpu.VMEM((SLOTS, TILE, TILE), jnp.bfloat16), matrix(BLK, BLK), matrix(2 * rows, BLK), matrix(2 * rows, BLK)],
        4 * 2 * rows * BLK * BLK,
        5 << 20,
        24,
    )
    left = kernel(
        left_kernel,
        "left",
        (inverse, weight_grad, w_core, w_0, w_1, w_2),
        [pltpu.VMEM] * 6,
        jax.ShapeDtypeStruct((2 * rows, BLK), jnp.float32),
        pltpu.VMEM,
        [matrix(BLK, BLK)],
        2 * 2 * rows * BLK * BLK,
        9 << 20,
        20,
    )
    full = kernel(
        spread_kernel,
        "spread",
        (first_own, first_got, second_own, second_got),
        [pltpu.VMEM] * 4,
        shaped(BLK, BLK),
        pltpu.VMEM,
        [],
        0,
        8 << 20,
        8,
    )
    theirs, mine = kernel(
        right_kernel,
        "right",
        (full, left, inverse, w_3),
        [pltpu.VMEM] * 4,
        [shaped(rows, BLK)] * 2,
        [pltpu.VMEM] * 2,
        [matrix(2 * rows, BLK)] * 3,
        6 * 2 * rows * BLK * BLK,
        8 << 20,
        24,
    )
    theirs = send(theirs, CORE, "out_core")
    out = jnp.zeros((rows, 2 * BLK), jnp.bfloat16)
    out = lax.dynamic_update_slice(out, mine, (0, core * BLK))
    return lax.dynamic_update_slice(out, theirs, (0, other))


def solution(mesh):
    return jax.shard_map(
        on_device,
        mesh=mesh,
        in_specs=(P("dp", None), P("dp", "tensor"), P("dp", "tensor")),
        out_specs=P("dp", "tensor"),
        check_vma=False,
    )
```
